32 devices in a mesh: row: 4 (over x, core), col: 8 (over z, y).
Axes of the slice: x: 2, y: 2, z: 4, core: 2. Of those that a mesh axis runs over, the one named last changes fastest.
Arguments:
- centroid: float32 [3, 131072], P(None, ('row', 'col')), may hold values from -6 to 6
- normals: float32 [3, 131072], P(None, ('row', 'col')), may hold values from -3 to 3
- tangent: float32 [3, 131072], P(None, ('row', 'col')), may hold values from -3 to 3
- element_area: float32 [131072], P(('row', 'col')), may hold values from 0.01 to 0.04
- forward_field: float32 [2, 131072], P(None, ('row', 'col')), may hold values from -6 to 6
- adjoint_field: float32 [2, 131072], P(None, ('row', 'col')), may hold values from -6 to 6
- corners: int32 [3, 131072], P(None, ('row', 'col')), may hold values from 0 to 65535, as said below
- slot_map: int32 [65536], replicated, may hold values from 0 to 65535, as said below
- quad_order: int32 [32, 4, 8, 32], P('row', None, 'col'), may hold values from 0 to 2
- morph_modes: float32 [300, 6, 65536], P(None, None, ('row', 'col')), may hold values from -0.3 to 0.3
Outputs:
- vertex_partial: float32 [6, 65536], P(None, ('row', 'col'))
- mode_gradient: float32 [300], replicated
The draws below stay inside these ranges and needn't reach their ends.
Inputs may be any that keep to these rules, and one draw needn't show every extreme that they name: slot_map is a permutation of 0 to 65535. `corners`: for each shard of elements (elements b * 4096 to (b + 1) * 4096 - 1), its 12288 corner references map through slot_map onto the slots of any one patch at most 384 times, and exactly 384 times for some patch.
All inputs are finite; a program needn't handle non-finite values.
Results may differ from the reference program's by a relative error of at most 0.0003.
Values sent between devices are 32-bit elements; how exact they have to be, the bound alone decides.
No kernel may reach another device: no remote copies, remote signals or barrier semaphores. Data moves between devices by JAX's collectives and lax.ppermute only.
A program may use at most 128 MiB of HBM per device.

```python
import math
import jax
import jax.numpy as jnp
from jax import lax

E = 131072
V = 65536
MODES = 300
TC = 128
SLAB_DEV = 8
EL = 4096
SLAB = 256
TILES = 32
N_ROW = 4
N_COL = 8
DEVICES = 32


def joint_layout(key):
    base_key = jax.random.fold_in(key, 7331)
    slot_key = jax.random.fold_in(base_key, 1)
    owner_key = jax.random.fold_in(base_key, 2)
    inside_key = jax.random.fold_in(base_key, 3)
    slot_table = jax.random.permutation(slot_key, V).astype(jnp.int32)
    shard_count = E // EL
    shard_keys = jax.random.split(owner_key, shard_count)

    def shard_owners(shard_key):
        order = jax.random.permutation(shard_key, shard_count).astype(jnp.int32)
        return order[jnp.arange(3 * EL, dtype=jnp.int32) % shard_count]
    owner_ids = jax.vmap(shard_owners)(shard_keys)
    inside_ids = jax.random.randint(inside_key, (shard_count, 3 * EL), 0, V // shard_count, dtype=jnp.int32)
    wanted_slot = owner_ids * (V // shard_count) + inside_ids
    inverse_table = jnp.argsort(slot_table, stable=True).astype(jnp.int32)
    vertex_ids = inverse_table[wanted_slot]
    corner_table = jnp.transpose(vertex_ids.reshape(shard_count, 3, EL), (1, 0, 2)).reshape(3, E)
    return (corner_table.astype(jnp.int32), slot_table)


def draw_corners(key, part):
    corner_table, slot_table = joint_layout(key)
    return corner_table


def draw_slot_map(key, part):
    corner_table, slot_table = joint_layout(key)
    return slot_table


def touch_ends(entries, stream_key, least, largest):
    index_at = [jax.random.randint(jax.random.fold_in(stream_key, axis), (), 0, length) for axis, length in enumerate(entries.shape)]
    main_axis = entries.shape.index(max(entries.shape))
    beside = index_at[:main_axis] + [(index_at[main_axis] + 1) % entries.shape[main_axis]] + index_at[main_axis + 1:]
    return entries.at[tuple(index_at)].set(least).at[tuple(beside)].set(largest)


def block_scale(rng, extent, shards, low, top_value):
    loudness, own = 1.0, jax.random.fold_in(rng, 6)
    for dim, parts in shards:
        draws = jnp.exp(jax.random.uniform(jax.random.fold_in(own, dim), (parts,), jnp.float32, low / len(shards), top_value / len(shards)))
        loudness = loudness * jnp.repeat(draws, extent[dim] // parts).reshape([-1 if axis == dim else 1 for axis in range(len(extent))])
    return loudness


def scatter_about(key, extent, width, most, pieces=(), kind=jnp.bfloat16):
    level = block_scale(key, extent, pieces, -0.22, 0.18) if pieces else 1.0
    values = jax.random.normal(key, extent, jnp.float32) * width * level
    return jnp.minimum(jnp.maximum(values, -most), most).astype(kind)


def setup_inputs(seed: int = 0) -> dict:
    seeds = jax.random.split(jax.random.key(seed), 11)
    return {
        "centroid": scatter_about(seeds[0], (3, E), 1.0, 6.0, ((1, 32),), jnp.float32),
        "normals": scatter_about(seeds[1], (3, E), 0.577, 3.0, ((1, 32),), jnp.float32),
        "tangent": scatter_about(seeds[2], (3, E), 0.577, 3.0, ((1, 32),), jnp.float32),
        "element_area": jnp.clip(jnp.exp(math.log(0.04) - 1.3862944 * jax.random.uniform(seeds[3], (E,), jnp.float32) ** block_scale(seeds[3], (E,), ((0, 32),), -0.2, 0.2)), 0.01, 0.04),
        "forward_field": scatter_about(seeds[4], (2, E), 1.0, 6.0, ((1, 32),), jnp.float32),
        "adjoint_field": scatter_about(seeds[5], (2, E), 1.0, 6.0, ((1, 32),), jnp.float32),
        "corners": draw_corners(jax.random.fold_in(seeds[10], 71), 0),
        "slot_map": draw_slot_map(jax.random.fold_in(seeds[10], 71), 0),
        "quad_order": touch_ends(jax.random.randint(seeds[8], (DEVICES, N_ROW, N_COL, TILES), 0, 3), jax.random.fold_in(seeds[8], 1), 0, 2).astype(jnp.int32),
        "morph_modes": scatter_about(seeds[9], (MODES, 6, V), 0.05, 0.3, ((2, 32),), jnp.float32),
    }


wavenumber = 4.0
quad_offsets = (-0.6, 0.0, 0.6)
quad_table = ((0.0, 1.0, 0.0), (0.5, 0.0, 0.5), (1.0 / 3.0, 1.0 / 3.0, 1.0 / 3.0))

def point_weights(pair_flags, point_index):
    weight_sum = jnp.zeros(pair_flags.shape, jnp.float32)
    for flag_level in range(3):
        chosen = jnp.where(pair_flags == flag_level, quad_table[flag_level][point_index], 0.0)
        weight_sum = weight_sum + chosen.astype(jnp.float32)
    return weight_sum

def pair_terms(row_point, row_adjoint, col_point, col_normal, col_tangent, col_area, col_forward, pair_flags):
    row_count = row_point.shape[1]
    col_count = col_point.shape[1]
    row_total = jnp.zeros((3, row_count), jnp.float32)
    col_total = jnp.zeros((3, col_count), jnp.float32)
    normal_total = jnp.zeros((3, col_count), jnp.float32)
    real_coupling = row_adjoint[0][:, None] * col_forward[0][None, :] + row_adjoint[1][:, None] * col_forward[1][None, :]
    imag_coupling = row_adjoint[0][:, None] * col_forward[1][None, :] - row_adjoint[1][:, None] * col_forward[0][None, :]
    spread = jnp.sqrt(col_area)
    for point_index in range(3):
        weight = point_weights(pair_flags, point_index) * col_area[None, :]
        source = col_point + quad_offsets[point_index] * spread[None, :] * col_tangent
        offset = row_point[:, :, None] - source[:, None, :]
        radius_sq = lax.optimization_barrier(jnp.sum(offset * offset, axis=0)) + col_area[None, :]
        radius = jnp.sqrt(radius_sq)
        phase_arg = wavenumber * radius
        cosine = jnp.cos(phase_arg)
        sine_part = jnp.sin(phase_arg)
        scale_three = 1.0 / (4.0 * math.pi * radius * radius_sq)
        scale_five = scale_three / radius_sq
        first_real = (-cosine - phase_arg * sine_part) * scale_three
        first_imag = (-sine_part + phase_arg * cosine) * scale_three
        poly_real = 3.0 - phase_arg * phase_arg
        poly_imag = -3.0 * phase_arg
        second_real = (cosine * poly_real - sine_part * poly_imag) * scale_five
        second_imag = (sine_part * poly_real + cosine * poly_imag) * scale_five
        along_normal = lax.optimization_barrier(jnp.sum(offset * col_normal[:, None, :], axis=0))
        combo_real = -first_imag / wavenumber - second_real * along_normal
        combo_imag = first_real / wavenumber - second_imag * along_normal
        coeff_first = (real_coupling * first_real - imag_coupling * first_imag) * weight
        coeff_second = (real_coupling * combo_real - imag_coupling * combo_imag) * weight
        position = coeff_second[None] * offset - coeff_first[None] * col_normal[:, None, :]
        row_total = row_total + lax.optimization_barrier(jnp.sum(position, axis=2))
        col_total = col_total - lax.optimization_barrier(jnp.sum(position, axis=1))
        normal_total = normal_total - lax.optimization_barrier(jnp.sum(coeff_first[None] * offset, axis=1))
    return (row_total, col_total, normal_total)

def reference(centroid, normals, tangent, element_area, forward_field, adjoint_field, corners, slot_map, quad_order, morph_modes):
    device_count = N_ROW * N_COL
    slab_index = (jnp.arange(device_count, dtype=jnp.int32)[:, None] * EL + jnp.arange(SLAB_DEV, dtype=jnp.int32)[None, :]).reshape(-1)
    row_point = centroid[:, slab_index]
    row_adjoint = adjoint_field[:, slab_index]

    def visit_block(row_carry, shard_index):
        col_start = (shard_index * EL).astype(jnp.int32)
        col_point = lax.dynamic_slice_in_dim(centroid, col_start, EL, 1)
        col_normal = lax.dynamic_slice_in_dim(normals, col_start, EL, 1)
        col_tangent = lax.dynamic_slice_in_dim(tangent, col_start, EL, 1)
        col_area = lax.dynamic_slice_in_dim(element_area, col_start, EL, 0)
        col_forward = lax.dynamic_slice_in_dim(forward_field, col_start, EL, 1)
        tile_flags = quad_order[:, shard_index // N_COL, shard_index % N_COL, :]
        pair_flags = jnp.repeat(jnp.repeat(tile_flags, SLAB_DEV, axis=0), TC, axis=1)
        row_total, col_total, normal_total = pair_terms(row_point, row_adjoint, col_point, col_normal, col_tangent, col_area, col_forward, pair_flags)
        return (row_carry + row_total, jnp.concatenate([col_total, normal_total], axis=0))
    row_sum, col_parts = lax.scan(visit_block, jnp.zeros((3, SLAB), jnp.float32), jnp.arange(device_count, dtype=jnp.int32))
    col_whole = jnp.transpose(col_parts, (1, 0, 2)).reshape(6, E)
    row_whole = jnp.pad(row_sum.reshape(3, device_count, SLAB_DEV), ((0, 3), (0, 0), (0, EL - SLAB_DEV))).reshape(6, E)
    element_part = col_whole + row_whole
    slot_ids = slot_map[corners].reshape(-1)
    values = jnp.concatenate([(element_part / 3.0).T] * 3, axis=0)
    vertex_partial = jax.ops.segment_sum(values, slot_ids, num_segments=V).T
    mode_gradient = jnp.dot(morph_modes.reshape(MODES, 6 * V), vertex_partial.reshape(6 * V), precision=lax.Precision.HIGHEST)
    return (vertex_partial, mode_gradient)
```

```python
import functools
import math

import jax
import jax.numpy as jnp
import numpy as np
from jax import lax
from jax.experimental import pallas as pl
from jax.experimental.pallas import tpu as pltpu
from jax.sharding import PartitionSpec as P

SLAB_DEV = 8
LANES = 128
WAVE = 4.0
OFFSET = 0.6
FLAG_WEIGHTS = (1.0, 0.5, 1.0 / 3.0)
GROUPS = (16, 8, 6)
F32 = jnp.float32
BF16 = jnp.bfloat16
AXES = ("row", "col")


def fit_even(fn, degree):
    series = np.polynomial.chebyshev.Chebyshev.interpolate(
        lambda u: fn(np.sqrt(np.maximum(u, 1e-30))), degree, domain=[0, 0.25]
    )
    return [float(x) for x in series.convert(kind=np.polynomial.Polynomial).coef]


SIN_HALF = fit_even(lambda f: math.sqrt(2) * np.sin(np.pi * f) / f, 3)
COS_HALF = fit_even(lambda f: math.sqrt(2) * np.cos(np.pi * f), 3)


def horner(coefs, u):
    total = coefs[-1] * u + coefs[-2]
    for c in coefs[-3::-1]:
        total = total * u + c
    return total


def iota(shape, dim):
    return lax.broadcasted_iota(jnp.int32, shape, dim)


def dot_lanes(a, b, **kw):
    return lax.dot_general(a, b, (((1,), (1,)), ((), ())), preferred_element_type=F32, **kw)


def split(x):
    high = x.astype(BF16)
    return high, (x - high.astype(F32)).astype(BF16)


def plan_kernel(devices, cap, corner_ref, table_ref, hp_ref, lp_ref, out_ref, slot, scat, order):
    count = corner_ref.shape[1]
    rows = table_ref.shape[0]
    patch = rows * LANES // devices
    tiles = -(-cap // LANES)
    table = table_ref[...]
    low = (table & 255).astype(F32)
    both = jnp.concatenate([(table.astype(F32) - low).T, low.T], axis=0).astype(BF16)
    width = min(1024, count)
    half = min(rows, 256)
    hi_iota = iota((half, width), 0).astype(F32).astype(BF16)
    lo_iota = iota((LANES, width), 0)
    for n in range(3):

        def look(i, carry, n=n):
            at = pl.ds(pl.multiple_of(i * width, LANES), width)
            c = corner_ref[n : n + 1, at]
            hi = (c >> 7).astype(F32)
            lo = c & 127
            hot = jnp.concatenate(
                [
                    jnp.where(hi_iota == (hi - float(g)).astype(BF16), 1.0, 0.0).astype(BF16)
                    for g in range(0, rows, half)
                ],
                axis=0,
            )
            found = jnp.dot(both, hot, preferred_element_type=F32)
            found = found[:LANES] + found[LANES:]
            slot[n : n + 1, at] = jnp.sum(
                jnp.where(lo_iota == lo, found, 0.0), axis=0, keepdims=True
            )
            return carry

        lax.fori_loop(0, count // width, look, 0)
    chunk = 256
    tri = jnp.where(iota((chunk, chunk), 0) <= iota((chunk, chunk), 1), 1.0, 0.0).astype(BF16)
    own_iota = iota((devices, chunk), 0).astype(F32)
    carry = jnp.zeros((devices, 1), F32)
    for n in range(3):
        for i in range(count // chunk):
            at = slice(i * chunk, (i + 1) * chunk)
            s = slot[n : n + 1, at]
            owner = jnp.floor((s + 0.5) * (1.0 / patch))
            mask = own_iota == owner
            pre = jnp.dot(
                jnp.where(mask, 1.0, 0.0).astype(BF16), tri, preferred_element_type=F32
            )
            rank = jnp.sum(jnp.where(mask, pre + carry, 0.0), axis=0, keepdims=True) - 1.0
            carry = carry + pre[:, chunk - 1 :]
            tile = jnp.floor((rank + 0.5) * (1.0 / LANES))
            pair = jnp.floor((owner + 0.5) * 0.5)
            hp_ref[n : n + 1, at] = pair * tiles + tile
            lp_ref[n : n + 1, at] = (owner - 2.0 * pair) * LANES + rank - tile * LANES
    units = devices // 2 * tiles
    unit_iota = iota((units, width), 0).astype(F32)
    lane_iota = iota((256, width), 0).astype(F32).astype(BF16)
    scat[...] = jnp.zeros(scat.shape, F32)
    for n in range(3):

        def put(i, carry, n=n):
            at = pl.ds(pl.multiple_of(i * width, LANES), width)
            s = slot[n : n + 1, at]
            inside = s - jnp.floor((s + 0.5) * (1.0 / patch)) * patch
            big = jnp.floor((inside + 0.5) * (1.0 / 256.0)) * 256.0
            mask = unit_iota == hp_ref[n : n + 1, at]
            lhs = jnp.concatenate(
                [jnp.where(mask, big, 0.0), jnp.where(mask, inside - big, 0.0)], axis=0
            ).astype(BF16)
            hot = jnp.where(lane_iota == lp_ref[n : n + 1, at].astype(BF16), 1.0, 0.0).astype(BF16)
            got = dot_lanes(lhs, hot)
            got = got[:units] + got[units:]
            scat[0] += got[:, :LANES]
            scat[1] += got[:, LANES:]
            return carry

        lax.fori_loop(0, count // width, put, 0)
    for b in range(2):
        for j in range(tiles):
            order[j, pl.ds(b, devices // 2, stride=2), :] = scat[
                b, pl.ds(j, devices // 2, stride=tiles), :
            ]
    for j in range(tiles):
        out_ref[:, j * LANES : (j + 1) * LANES] = order[j]
    lane = iota((1, LANES), 1)
    slab = slot[0:1, 0:LANES]
    for n in (1, 2):
        slab = jnp.where(
            lane < n * SLAB_DEV, slab, pltpu.roll(slot[n : n + 1, 0:LANES], n * SLAB_DEV, 1)
        )
    out_ref[:, tiles * LANES :] = jnp.broadcast_to(slab, (devices, LANES))


def plan(corners, table, devices, cap):
    count = corners.shape[1]
    tiles = -(-cap // LANES)
    return pl.pallas_call(
        functools.partial(plan_kernel, devices, cap),
        out_shape=(
            jax.ShapeDtypeStruct((3, count), F32),
            jax.ShapeDtypeStruct((3, count), F32),
            jax.ShapeDtypeStruct((devices, (tiles + 1) * LANES), F32),
        ),
        scratch_shapes=[
            pltpu.VMEM((3, count), F32),
            pltpu.VMEM((2, devices // 2 * tiles, LANES), F32),
            pltpu.VMEM((tiles, devices, LANES), F32),
        ],
        compiler_params=pltpu.CompilerParams(vmem_limit_bytes=24 << 20),
        name="plan",
    )(corners, table)


def point(dist_sq, normal_dot, cr, ci):
    inv = lax.rsqrt(dist_sq)
    turns = (dist_sq * inv) * (0.5 / math.pi)
    inv_sq3 = (inv * 3.0) * inv
    frac = turns - jnp.round(turns)
    u = frac * frac
    s = frac * horner(SIN_HALF, u)
    c = horner(COS_HALF, u)
    er = inv_sq3 - (s * s) * inv_sq3
    ei = (s * c) * inv_sq3
    wr = cr * er - ci * ei
    wi = cr * ei + ci * er
    near = wr * inv
    a = near + wi
    b = (wi * inv - wr) + normal_dot * (near - a * inv_sq3)
    return a, b


def work_list(flags, ids_ref, devices):
    ones = jnp.concatenate([jnp.where(flags == f, 1.0, 0.0) for f in range(3)], axis=0)
    ii = iota((LANES, LANES), 0)
    tri = jnp.where(ii < iota((LANES, LANES), 1), 1.0, 0.0).astype(BF16)
    before = jnp.dot(ones.astype(BF16), tri, preferred_element_type=F32)
    total = jnp.dot(ones.astype(BF16), jnp.ones((LANES, LANES), BF16), preferred_element_type=F32)
    run = jnp.zeros((1, LANES), F32)
    place = jnp.zeros((8, LANES), F32)
    row = iota((8, LANES), 0)
    bounds = []
    for f, size in enumerate(GROUPS):
        start = run
        offset = jnp.zeros((8, LANES), F32)
        for r in range(8):
            offset = jnp.where(row == r, run, offset)
            run = run + total[f * 8 + r : f * 8 + r + 1]
        steps = jnp.floor((run - start + (size - 0.5)) * (1.0 / size))
        bounds += [start, steps]
        run = start + steps * size
        place = place + ones[f * 8 : f * 8 + 8] * (before[f * 8 : f * 8 + 8] + offset)
    place = place.astype(jnp.int32)
    hi, lo = place >> 7, place & 127
    hi_iota = iota((16, LANES), 0)
    got = jnp.zeros((32, LANES), F32)
    for r in range(8):
        hot = jnp.where(ii == lo[r : r + 1], 1.0, 0.0).astype(BF16)
        mask = hi_iota == hi[r : r + 1]
        lhs = jnp.concatenate(
            [jnp.where(mask, ids_ref[k, r : r + 1, :], 0.0) for k in range(2)], axis=0
        )
        got = got + dot_lanes(lhs.astype(BF16), hot)
    shard = got[:16].astype(jnp.int32)
    bounds = [b.astype(jnp.int32) for b in bounds] + [jnp.zeros((2, LANES), jnp.int32)]
    return (
        jnp.where(shard == 0, devices, shard - 1),
        got[16:].astype(jnp.int32),
        jnp.concatenate(bounds, axis=0),
    )


def pair_kernel(
    mesh_shape,
    tiles,
    col_ref,
    inbox_ref,
    ids_ref,
    centroid_ref,
    normals_ref,
    tangent_ref,
    area_ref,
    forward_ref,
    val_ref,
    row_ref,
    tgt,
    src,
    col,
    row,
    list_vmem,
    todo,
    sem,
):
    n_row, n_col = mesh_shape
    devices = n_row * n_col
    mine = col_ref[0]
    flag_rows = 8 // n_row
    flags = []
    for r in range(n_row):
        block = inbox_ref[r * n_col : (r + 1) * n_col, LANES : (1 + flag_rows) * LANES]
        block = jnp.where(iota(block.shape, 0) == mine, block, 0.0)
        block = jnp.sum(block, axis=0, keepdims=True)
        flags += [block[:, h * LANES : (h + 1) * LANES] for h in range(flag_rows)]
    flags = jnp.concatenate(flags, axis=0)
    shard, tile, bounds = work_list(flags, ids_ref, devices)
    list_vmem[0:16, :] = shard
    list_vmem[16:32, :] = tile
    list_vmem[32:40, :] = bounds
    copy = pltpu.make_async_copy(list_vmem, todo, sem)
    copy.start()
    words = inbox_ref[:, 0:LANES].T
    for d in range(devices):
        for k in range(5):
            w = words[k * 8 : k * 8 + 8, d : d + 1] * (WAVE if k < 3 else 1.0)
            tgt[d, k] = jnp.broadcast_to(w, (8, LANES))
    zero = jnp.zeros((8, LANES), F32)
    for k in range(5):
        tgt[devices, k] = zero

    def prepare(t, carry):
        at = pl.ds(pl.multiple_of(t * LANES, LANES), LANES)

        def load(ref, k):
            return jnp.broadcast_to(ref[k : k + 1, at], (8, LANES))

        area = jnp.broadcast_to(area_ref[pl.ds(t, 1), :], (8, LANES))
        spread = jnp.sqrt(area) * (WAVE * OFFSET)
        u = [load(tangent_ref, k) * spread for k in range(3)]
        n = [load(normals_ref, k) * (WAVE * WAVE) for k in range(3)]
        for k in range(3):
            src[t, k] = load(centroid_ref, k) * WAVE
            src[t, 3 + k] = n[k]
            src[t, 6 + k] = u[k]
        src[t, 9] = area * (WAVE * WAVE)
        src[t, 10] = u[0] * u[0] + u[1] * u[1] + u[2] * u[2]
        src[t, 11] = u[0] * n[0] + u[1] * n[1] + u[2] * n[2]
        scale = area * (WAVE**3 / (4.0 * math.pi) / 3.0)
        src[t, 12] = load(forward_ref, 0) * scale
        src[t, 13] = load(forward_ref, 1) * scale
        for k in range(9):
            col[t, k] = zero
        return carry

    lax.fori_loop(0, tiles, prepare, 0)

    def clear(d, carry):
        for k in range(3):
            row[d, k] = zero
        return carry

    lax.fori_loop(0, devices + 1, clear, 0)
    copy.wait()
    for f, size in enumerate(GROUPS):
        start = todo[32 + 2 * f, 0]

        def step(i, carry, f=f, size=size, start=start):
            for g in range(size):
                p = start + i * size + g
                d = todo[p >> 7, p & 127]
                t = todo[16 + (p >> 7), p & 127]
                diff = [tgt[d, k] - src[t, k] for k in range(3)]
                dist = diff[0] * diff[0] + diff[1] * diff[1] + diff[2] * diff[2] + src[t, 9]
                n = [src[t, 3 + k] for k in range(3)]
                along = diff[0] * n[0] + diff[1] * n[1] + diff[2] * n[2]
                ar, ai = tgt[d, 3], tgt[d, 4]
                if f:
                    ar = ar * FLAG_WEIGHTS[f]
                    ai = ai * FLAG_WEIGHTS[f]
                fr, fi = src[t, 12], src[t, 13]
                cr = ar * fr + ai * fi
                ci = ar * fi - ai * fr
                if f == 0:
                    sa, sb = point(dist, along, cr, ci)
                else:
                    u = [src[t, 6 + k] for k in range(3)]
                    cross = diff[0] * u[0] + diff[1] * u[1] + diff[2] * u[2]
                    cross = cross + cross
                    base = dist + src[t, 10]
                    a0, b0 = point(base + cross, along + src[t, 11], cr, ci)
                    a2, b2 = point(base - cross, along - src[t, 11], cr, ci)
                    sa, sb, da, db = a0 + a2, b0 + b2, a0 - a2, b0 - b2
                    if f == 2:
                        a1, b1 = point(dist, along, cr, ci)
                        sa, sb = sa + a1, sb + b1
                moved = [sb * diff[k] for k in range(3)]
                for k in range(3):
                    col[t, k] += moved[k]
                    col[t, 3 + k] += sa * diff[k]
                col[t, 6] += sa
                if f:
                    col[t, 7] += db
                    col[t, 8] += da
                for k in range(3):
                    part = moved[k] + sa * n[k]
                    if f:
                        part = part + db * u[k]
                    row[d, k] += part
            return carry

        lax.fori_loop(0, todo[33 + 2 * f, 0], step, 0)
    scale_p = 1.0 / (3.0 * WAVE * WAVE)
    scale_n = 1.0 / (3.0 * WAVE)

    def finish(t, carry):
        at = pl.ds(pl.multiple_of(t * LANES, LANES), LANES)
        s = [jnp.sum(col[t, k], axis=0, keepdims=True) for k in range(9)]
        for k in range(3):
            u = src[t, 6 + k, 0:1]
            n = src[t, 3 + k, 0:1]
            val_ref[k : k + 1, at] = (s[k] + u * s[7] + n * s[6]) * -scale_p
            val_ref[3 + k : 4 + k, at] = (s[3 + k] + u * s[8]) * scale_n
        return carry

    lax.fori_loop(0, tiles, finish, 0)
    ones = jnp.full((8, LANES), scale_p, F32)
    for k in range(3):
        sums = dot_lanes(
            ones, row[0:devices, k].reshape(devices * 8, LANES), precision=lax.Precision.HIGHEST
        )
        row_ref[k : k + 1, :] = sums[0:1]


def pairs(mesh_shape, mine, inbox, centroid, normals, tangent, area, forward):
    n_row, n_col = mesh_shape
    devices = n_row * n_col
    count = centroid.shape[1]
    tiles = count // LANES
    word = np.arange(devices * tiles)
    per_row = devices // n_row
    ids = np.stack([word // tiles + 1, word % tiles]).astype(np.float32).reshape(2, 8, LANES)
    assert per_row * tiles * n_row == 8 * LANES
    vmem = pl.BlockSpec(memory_space=pltpu.VMEM)
    return pl.pallas_call(
        functools.partial(pair_kernel, mesh_shape, tiles),
        in_specs=[pl.BlockSpec(memory_space=pltpu.SMEM)] + [vmem] * 7,
        out_shape=(
            jax.ShapeDtypeStruct((6, count), F32),
            jax.ShapeDtypeStruct((3, SLAB_DEV * devices), F32),
        ),
        scratch_shapes=[
            pltpu.VMEM((devices + 1, 5, 8, LANES), F32),
            pltpu.VMEM((tiles, 14, 8, LANES), F32),
            pltpu.VMEM((tiles, 9, 8, LANES), F32),
            pltpu.VMEM((devices + 1, 3, 8, LANES), F32),
            pltpu.VMEM((40, LANES), jnp.int32),
            pltpu.SMEM((40, LANES), jnp.int32),
            pltpu.SemaphoreType.DMA(()),
        ],
        compiler_params=pltpu.CompilerParams(vmem_limit_bytes=24 << 20),
        name="pairs",
    )(mine, inbox, jnp.asarray(ids), centroid, normals, tangent, area, forward)


def bucket_kernel(devices, cap, rows, val_ref, part_ref, hp_ref, lp_ref, out_ref, acc):
    count = val_ref.shape[1]
    tiles = -(-cap // LANES)
    units = devices // 2 * tiles
    width = min(1024, count)
    acc[...] = jnp.zeros(acc.shape, F32)
    lane_iota = iota((256, width), 0).astype(F32).astype(BF16)
    unit = (iota((16, width), 0) >> 3).astype(F32).astype(BF16)
    for n in range(3):

        def put(i, carry, n=n):
            at = pl.ds(pl.multiple_of(i * width, LANES), width)
            v = val_ref[:, at]
            v = jnp.concatenate([v, jnp.zeros((2, width), F32)], axis=0)
            v = jnp.concatenate([v, v], axis=0)
            high, low = split(v)
            hp = hp_ref[n : n + 1, at]
            masks = [unit == (hp - 2.0 * q).astype(BF16) for q in range(units // 2)]
            zero = jnp.zeros((16, width), BF16)
            lhs = jnp.concatenate(
                [jnp.where(m, part, zero) for part in (high, low) for m in masks], axis=0
            )
            hot = jnp.where(lane_iota == lp_ref[n : n + 1, at].astype(BF16), 1.0, 0.0).astype(BF16)
            acc[...] += dot_lanes(lhs, hot)
            return carry

        lax.fori_loop(0, count // width, put, 0)
    packed = 2 * tiles * LANES == part_ref.shape[0] * part_ref.shape[1]
    row = iota((8, LANES), 0)
    for j in range(tiles):
        if packed:
            part = jnp.where(
                row == 6,
                part_ref[j : j + 1, 0:LANES],
                part_ref[j : j + 1, LANES : 2 * LANES],
            )
        for o in range(devices):
            q = ((o // 2) * tiles + j) * 8
            lanes = slice((o % 2) * LANES, (o % 2 + 1) * LANES)
            got = acc[q : q + 8, lanes] + acc[units * 8 + q : units * 8 + q + 8, lanes]
            if packed:
                got = jnp.where(row < 6, got, part)
            out_ref[o, j * 8 : j * 8 + 8, :] = got
    if not packed:
        for r in range(rows - 8 * tiles):
            per = part_ref.shape[1] // LANES
            c, h = r // per, r % per
            line = part_ref[c : c + 1, h * LANES : (h + 1) * LANES]
            for o in range(devices):
                out_ref[o, 8 * tiles + r : 8 * tiles + r + 1, :] = line


def message_rows(devices, cap):
    tiles = -(-cap // LANES)
    extra = 3 * SLAB_DEV * devices // LANES
    return 8 * tiles + (0 if extra == 2 * tiles else extra)


def bucket(val, part, hp, lp, devices, cap):
    tiles = -(-cap // LANES)
    rows = message_rows(devices, cap)
    return pl.pallas_call(
        functools.partial(bucket_kernel, devices, cap, rows),
        out_shape=jax.ShapeDtypeStruct((devices, rows, LANES), F32),
        scratch_shapes=[pltpu.VMEM((devices // 2 * tiles * 16, 256), F32)],
        compiler_params=pltpu.CompilerParams(vmem_limit_bytes=32 << 20),
        name="bucket",
    )(val, part, hp, lp)


def owner_kernel(
    devices, cap, me_ref, inbox_ref, slots_ref, morph_ref, vertex_ref, out_ref, lhs, rhs, lines
):
    patch = vertex_ref.shape[1]
    modes = morph_ref.shape[0]
    tiles = -(-cap // LANES)
    his = patch // 256
    me = me_ref[0]
    lane_iota = iota((256, LANES), 0).astype(F32).astype(BF16)
    unit = (iota((16, LANES), 0) >> 3).astype(F32)
    zero = jnp.zeros((16, LANES), BF16)

    def place(k, v, inside):
        hi = jnp.floor((inside + 0.5) * (1.0 / 256.0))
        hot = jnp.where(lane_iota == (inside - hi * 256.0).astype(BF16), 1.0, 0.0)
        at = pl.ds(pl.multiple_of(k * LANES, LANES), LANES)
        rhs[:, at] = hot.astype(BF16)
        high, low = split(jnp.concatenate([v, v], axis=0))
        for q in range(his // 2):
            mask = unit == hi - 2.0 * q
            lhs[q * 16 : q * 16 + 16, at] = jnp.where(mask, high, zero)
            lhs[his * 8 + q * 16 : his * 8 + q * 16 + 16, at] = jnp.where(mask, low, zero)

    packed = inbox_ref.shape[1] == 8 * tiles
    wide = SLAB_DEV * devices // LANES

    def source(block, sums):
        around = pl.ds(pl.multiple_of(block * 8, 8), 8)
        inside = [slots_ref[around, j * LANES : (j + 1) * LANES] for j in range(tiles)]
        if cap % LANES:
            lane = iota((8, LANES), 1)
            inside = [jnp.where(lane < cap - j * LANES, x, -1.0) for j, x in enumerate(inside)]
        for r in range(8):
            s = block * 8 + r
            for j in range(tiles):
                place(s * tiles + j, inbox_ref[s, j * 8 : j * 8 + 8, :], inside[j][r : r + 1])
            if packed:
                sums = tuple(x + inbox_ref[s, j * 8 : j * 8 + 8, :] for j, x in enumerate(sums))
            else:
                sums = (sums[0] + inbox_ref[s, 8 * tiles :, :],)
        return sums

    if packed:
        sums = tuple(jnp.zeros((8, LANES), F32) for _ in range(tiles))
    else:
        sums = (jnp.zeros((3 * wide, LANES), F32),)
    sums = lax.fori_loop(0, devices // 8, source, sums)
    own = slots_ref[:, tiles * LANES : (tiles + 1) * LANES]
    big = jnp.floor((own + 0.5) * (1.0 / 256.0))
    own = jnp.concatenate([big, own - 256.0 * big], axis=0).astype(BF16)
    word = iota((LANES, SLAB_DEV * devices), 0)
    lane = iota((LANES, SLAB_DEV * devices), 1)
    here = iota((devices, SLAB_DEV * devices), 0) == (
        iota((devices, SLAB_DEV * devices), 1) // SLAB_DEV
    )
    base = (me * patch).astype(F32)
    for n in range(3):
        pick = jnp.where(word == n * SLAB_DEV + lane % SLAB_DEV, 1.0, 0.0).astype(BF16)
        got = jnp.dot(own, pick, preferred_element_type=F32)
        got = got[:devices] * 256.0 + got[devices:]
        slot = jnp.sum(jnp.where(here, got, 0.0), axis=0, keepdims=True) - base
        for h in range(wide):
            lines_v = []
            for c in range(3):
                if packed:
                    lines_v.append(sums[c][6 + h : 7 + h])
                else:
                    lines_v.append(sums[0][c * wide + h : c * wide + h + 1])
            v = jnp.concatenate(lines_v + [jnp.zeros((5, LANES), F32)], axis=0)
            place(devices * tiles + n * wide + h, v, slot[:, h * LANES : (h + 1) * LANES])
    both = dot_lanes(lhs[...], rhs[...])
    both = both[: his * 8] + both[his * 8 :]
    for q in range(his):
        vertex_ref[:, q * 256 : (q + 1) * 256] = both[q * 8 : q * 8 + 6]

    lines[...] = jnp.zeros(lines.shape, F32)
    vert = [vertex_ref[:, q * LANES : (q + 1) * LANES] for q in range(patch // LANES)]

    def project(m, carry):
        terms = [morph_ref[m, :, q * LANES : (q + 1) * LANES] * v for q, v in enumerate(vert)]
        while len(terms) > 1:
            terms = [a + b for a, b in zip(terms[::2], terms[1::2])]
        lines[pl.ds(m, 1), :] = jnp.sum(terms[0], axis=0, keepdims=True)
        return carry

    lax.fori_loop(0, modes, project, 0, unroll=4)
    ones = jnp.ones((8, LANES), F32)
    sums = dot_lanes(ones, lines[...], precision=lax.Precision.HIGHEST)
    for o in range(0, devices, 8):
        out_ref[o : o + 8, :] = sums


def owner(me, inbox, slots, morph, devices, cap):
    modes, _, patch = morph.shape
    tiles = -(-cap // LANES)
    depth = (devices * tiles + 3 * SLAB_DEV * devices // LANES) * LANES
    words = -(-modes // LANES) * LANES
    vmem = pl.BlockSpec(memory_space=pltpu.VMEM)
    return pl.pallas_call(
        functools.partial(owner_kernel, devices, cap),
        in_specs=[pl.BlockSpec(memory_space=pltpu.SMEM), vmem, vmem, vmem],
        out_shape=(
            jax.ShapeDtypeStruct((6, patch), F32),
            jax.ShapeDtypeStruct((devices, words), F32),
        ),
        scratch_shapes=[
            pltpu.VMEM((patch // 256 * 16, depth), BF16),
            pltpu.VMEM((256, depth), BF16),
            pltpu.VMEM((words, LANES), F32),
        ],
        compiler_params=pltpu.CompilerParams(vmem_limit_bytes=48 << 20),
        name="owner",
    )(me, inbox, slots, morph)


def swap(x):
    return lax.all_to_all(x, AXES, split_axis=0, concat_axis=0, tiled=True)


def body(
    centroid,
    normals,
    tangent,
    element_area,
    forward_field,
    adjoint_field,
    corners,
    slot_map,
    quad_order,
    morph_modes,
):
    n_row, n_col = lax.axis_size("row"), lax.axis_size("col")
    devices = n_row * n_col
    count = centroid.shape[1]
    cap = -(-3 * count // devices)
    mine = lax.axis_index("col").astype(jnp.int32).reshape(1)
    me = lax.axis_index(AXES).astype(jnp.int32).reshape(1)

    slab = jnp.concatenate([centroid[:, :SLAB_DEV], adjoint_field[:, :SLAB_DEV]], axis=0)
    slab = jnp.pad(slab.reshape(-1), (0, LANES - 5 * SLAB_DEV))
    flags = jnp.transpose(quad_order[:, :, 0, :], (1, 0, 2)).reshape(n_row, 1, -1).astype(F32)
    flags = jnp.broadcast_to(flags, (n_row, n_col, flags.shape[2])).reshape(devices, -1)
    first = jnp.concatenate([jnp.broadcast_to(slab[None], (devices, LANES)), flags], axis=1)
    first = swap(first)

    hp, lp, slots = plan(corners, slot_map.reshape(-1, LANES), devices, cap)
    slots = swap(slots)

    val, part = pairs(
        (n_row, n_col),
        mine,
        first,
        centroid,
        normals,
        tangent,
        element_area.reshape(-1, LANES),
        forward_field,
    )
    inbox = swap(bucket(val, part, hp, lp, devices, cap))
    vertex_partial, sums = owner(me, inbox, slots, morph_modes, devices, cap)
    mode_gradient = jnp.sum(swap(sums), axis=0)[: morph_modes.shape[0]]
    return (vertex_partial, mode_gradient)


def solution(mesh):
    return jax.shard_map(
        body,
        mesh=mesh,
        in_specs=(
            P(None, ("row", "col")),
            P(None, ("row", "col")),
            P(None, ("row", "col")),
            P(("row", "col")),
            P(None, ("row", "col")),
            P(None, ("row", "col")),
            P(None, ("row", "col")),
            P(),
            P("row", None, "col", None),
            P(None, None, ("row", "col")),
        ),
        out_specs=(P(None, ("row", "col")), P()),
        check_vma=False,
    )
```
